32 devices in a mesh: groups: 2 (over y), region: 4 (over z), slab: 2 (over x), chip: 2 (over core).
Axes of the slice: x: 2, y: 2, z: 4, core: 2. Of those that a mesh axis runs over, the one named last changes fastest.
Arguments:
- features: bfloat16 [16384, 256], P(('groups', 'region', 'slab', 'chip')), parts along dimension 0, may hold values from -6 to 6
- neighbours: int32 [27, 16384], P(None, ('groups', 'region', 'slab', 'chip')), parts along dimension 1, may hold values from -1 to 1279, as said below
- fetch_table: int32 [8, 2, 2, 4, 2], P('groups', 'slab', 'chip'), parts along dimension 0, may hold values from -1 to 7, as said below
- hilbert_slot: int32 [256], P(('groups', 'region', 'slab', 'chip')), parts along dimension 0, may hold values from 0 to 31, as said below
- patch_ids: int32 [16384], P(('groups', 'region', 'slab')), parts along dimension 0, may hold values from 0 to 7, never falling along the last dimension, each value on 1 to 2048 neighbouring positions
- conv_weight: bfloat16 [27, 256, 256], P(None, None, 'chip'), may hold values from -0.078125 to 0.078125
- cpe_weight: bfloat16 [256, 256], replicated, may hold values from -0.375 to 0.375
- cpe_bias: float32 [256], replicated, may hold values from -4 to 4
- cpe_gain: float32 [256], replicated, may hold values from 0.1 to 1.9
- cpe_shift: float32 [256], replicated, may hold values from -3 to 3
- norm1_gain: float32 [256], replicated, may hold values from 0.1 to 1.9
- norm1_shift: float32 [256], replicated, may hold values from -3 to 3
- query_weight: bfloat16 [256, 256], replicated, as said below
- pair_weight: bfloat16 [256, 512], replicated, as said below
- proj_weight: bfloat16 [256, 256], replicated, may hold values from -0.375 to 0.375
- norm2_gain: float32 [256], replicated, may hold values from 0.1 to 1.9
- norm2_shift: float32 [256], replicated, may hold values from -3 to 3
- fc1_weight: bfloat16 [256, 1024], replicated, may hold values from -0.375 to 0.375
- fc1_bias: float32 [1024], replicated, may hold values from -3 to 3
- fc2_weight: bfloat16 [1024, 256], replicated, may hold values from -0.1875 to 0.1875
Outputs:
- block_output: bfloat16 [16384, 256], P(('groups', 'region', 'slab', 'chip')), parts along dimension 0
The draws below stay inside these ranges and needn't reach their ends.
There are 2 independent parts, one for each index of `groups`. The reference program is written for one: setup_inputs(seed, part) draws one part's arguments, and reference() takes and returns one part's arrays. A program takes and returns all parts, laid end to end along the dimension named above; an argument that names none is the same for every part. Nothing has to cross between parts.
Inputs may be any that keep to these rules, and one draw needn't show every extreme that they name: `neighbours`: indices into the device's pool; offset 27 // 2 is always the point itself, at pool index 128 plus its row on the device. `fetch_table`: block indices on the source device. `hilbert_slot`: for each slab and chip index, the values on the 4 devices of that index form a permutation of 0 .. 31; one device sends either exactly 4 blocks or none to each region. `query_weight`: real entries of magnitude at most 100 over the fan-in's square root. `pair_weight`: real entries of order 1 over the fan-in's square root.
All inputs are finite; a program needn't handle non-finite values.
Results may differ from the reference program's by a relative error of at most 0.012.
The reference program's roundings to bfloat16 on the way count: a program that leaves them out, or rounds other values in their place, can miss the bound.
Values may be sent and summed in bfloat16 or wider, within the bound.
A program may use at most 64 MiB of HBM per device.

```python
import math
import jax
import jax.numpy as jnp
import numpy as np
from jax import lax

C = 256
FFN = 1024
PATCH = 1024
HEAD_DIM = 16
BLOCK = 64
OFFSETS = 27
HALO_B = 2
FETCH_CAP = 2
CAP = 4
POOL = 1280
POINTS = 8192
SCENES = 8
N_REGION = 4
N_SLAB = 2
N_CHIP = 2


def shared_keys(key):
    return jax.random.truncated_normal(key, -4.0, 4.0, (C, C), jnp.float32) * C ** (-0.5)


def draw_pair_weight(key, part):
    base = shared_keys(key)
    key = jax.random.fold_in(key, 14)
    values = jax.random.truncated_normal(key, -4.0, 4.0, (C, C), jnp.float32) * C ** (-0.5)
    return jnp.concatenate([base, values], axis=1).astype(jnp.bfloat16)


def draw_query_weight(key, part):
    key = jax.random.fold_in(key, 15)
    own = jax.random.truncated_normal(key, -4.0, 4.0, (C, C), jnp.float32) * C ** (-0.5)
    weight = own
    return weight.astype(jnp.bfloat16)


def draw_neighbours(key, part):
    key = jax.random.fold_in(key, 13)
    first, second = jax.random.split(key)
    index = jax.random.randint(first, (OFFSETS, POINTS), 0, POOL, dtype=jnp.int32)
    keep = jax.random.randint(second, (OFFSETS, POINTS), 0, 4, dtype=jnp.int32) > 0
    table = jnp.where(keep, index, -1)
    rows_dev = PATCH // N_CHIP
    centre = HALO_B * BLOCK + jnp.arange(POINTS, dtype=jnp.int32) % rows_dev
    table = table.at[OFFSETS // 2].set(centre)
    table = table.at[0, 0].set(POOL - 1)
    table = table.at[0, 1].set(-1)
    return table.astype(jnp.int32)


def draw_fetch_table(key, part):
    key = jax.random.fold_in(key, 12)
    first, second = jax.random.split(key)
    count = PATCH // N_CHIP // BLOCK
    shape = (N_REGION, N_SLAB, N_CHIP, N_REGION, FETCH_CAP)
    index = jax.random.randint(first, shape, 0, count, dtype=jnp.int32)
    keep = jax.random.randint(second, shape, 0, 2, dtype=jnp.int32)
    table = jnp.where(keep == 1, index, -1)
    table = table.at[0, 0, 0, 0, 0].set(count - 1)
    table = table.at[0, 0, 0, 1, 0].set(-1)
    return table.astype(jnp.int32)


def draw_hilbert_slot(key, part):
    key = jax.random.fold_in(key, 11)
    count = PATCH // N_CHIP // BLOCK
    per_source = count // CAP
    classes = N_SLAB * N_CHIP

    def one_class(class_key):
        first, second, third = jax.random.split(class_key, 3)
        shifts = jax.random.permutation(first, N_REGION)[:per_source].astype(jnp.int32)
        entry = jnp.arange(count, dtype=jnp.int32)
        target = (jnp.arange(N_REGION, dtype=jnp.int32)[:, None] + shifts[entry // CAP][None, :]) % N_REGION
        arrival = jax.vmap(lambda item: jax.random.permutation(item, count))(jax.random.split(second, N_REGION)).astype(jnp.int32)
        slot = arrival[target, jnp.broadcast_to(entry[None, :], target.shape)]
        placed = target * count + slot
        order = jax.vmap(lambda item: jax.random.permutation(item, count))(jax.random.split(third, N_REGION)).astype(jnp.int32)
        return jnp.take_along_axis(placed, order, axis=1)
    table = jax.vmap(one_class)(jax.random.split(key, classes))
    table = table.reshape(N_SLAB, N_CHIP, N_REGION, count).transpose(2, 0, 1, 3)
    return table.reshape(-1).astype(jnp.int32)


def steps_of(stream_key, dims, cuts, smallest, high):
    level, own = 1.0, jax.random.fold_in(stream_key, 6)
    for axis_at, shards_of in cuts:
        draws = jnp.exp(jax.random.uniform(jax.random.fold_in(own, axis_at), (shards_of,), jnp.float32, smallest / len(cuts), high / len(cuts)))
        level = level * jnp.repeat(draws, dims[axis_at] // shards_of).reshape([-1 if axis == axis_at else 1 for axis in range(len(dims))])
    return level


def length_profile(count, total, reach, skew):
    loads = [(1 << 20) // math.isqrt(grade ** skew) + 1 for grade in range(2, count + 1)]
    surplus, holding = total - reach - (count - 1), [1] * (count - 1)
    while surplus > 0:
        movable = [i for i in range(count - 1) if holding[i] < reach]
        whole, budget = sum([loads[i] for i in movable]), surplus
        for i in movable:
            addition = min(reach - holding[i], max(1, budget * loads[i] // whole), surplus)
            holding[i] = holding[i] + addition
            surplus = surplus - addition
    return np.array([reach] + holding)


def ragged(rng, number_of, total, limit, slope):
    if number_of == 2:
        one = jax.random.randint(rng, (), max(1, total - limit), min(limit, total - 1) + 1)
        return jnp.stack([one, total - one])
    sizes = jnp.asarray(length_profile(number_of, total, limit, slope), jnp.int32)
    twos = (number_of - 1) // 2
    donor, taker = sizes[1:1 + 2 * twos:2], sizes[2:2 + 2 * twos:2]
    room = jnp.minimum(donor - 1, limit - taker)
    shifted = jax.random.randint(jax.random.fold_in(rng, 1), (twos,), 0, 1 << 20) % (room + 1)
    sizes = sizes.at[1:1 + 2 * twos:2].set(donor - shifted).at[2:2 + 2 * twos:2].set(taker + shifted)
    return sizes[jax.random.permutation(jax.random.fold_in(rng, 2), number_of)]


def gaussian(rng, extent, width, reach, cuts=(), held_as=jnp.bfloat16):
    entries = jax.random.normal(rng, extent, jnp.float32) * width
    if len(cuts) > 0:
        entries = steps_of(rng, extent, cuts, -0.22, 0.18) * entries
    return jnp.clip(entries, min=-reach, max=reach).astype(held_as)


def setup_inputs(seed: int = 0, part: int = 0) -> dict:
    key_of = jax.random.split(jax.random.key(seed), 21)
    own_keys = jax.random.split(jax.random.fold_in(key_of[20], part), 21)
    features = gaussian(own_keys[0], (POINTS, C), 1.0, 6.0, ((0, 16),))
    neighbours = draw_neighbours(jax.random.fold_in(jax.random.fold_in(key_of[20], part), 71), part)
    fetch_table = draw_fetch_table(jax.random.fold_in(jax.random.fold_in(key_of[20], part), 71), part)
    hilbert_slot = draw_hilbert_slot(jax.random.fold_in(jax.random.fold_in(key_of[20], part), 71), part)
    patch_ids = jnp.searchsorted(jnp.cumsum(ragged(own_keys[4], SCENES, POINTS, 2 * PATCH, 1)), jnp.arange(POINTS), side="right").astype(jnp.int32)
    conv_weight = gaussian(key_of[5], (OFFSETS, C, C), (OFFSETS * C) ** -0.5, 0.078125, ((2, 2),))
    cpe_weight = gaussian(key_of[6], (C, C), C ** -0.5, 0.375)
    cpe_bias = gaussian(key_of[7], (C,), 1.0, 4.0, (), jnp.float32)
    cpe_gain = jnp.clip(1.0 + 0.18 * jax.random.normal(key_of[8], (C,), jnp.float32), 0.1, 1.9)
    cpe_shift = gaussian(key_of[9], (C,), 0.5, 3.0, (), jnp.float32)
    norm1_gain = jnp.clip(1.0 + 0.18 * jax.random.normal(key_of[10], (C,), jnp.float32), 0.1, 1.9)
    norm1_shift = gaussian(key_of[11], (C,), 0.5, 3.0, (), jnp.float32)
    query_weight = draw_query_weight(jax.random.fold_in(key_of[20], 71), part)
    pair_weight = draw_pair_weight(jax.random.fold_in(key_of[20], 71), part)
    proj_weight = gaussian(key_of[14], (C, C), C ** -0.5, 0.375)
    norm2_gain = jnp.clip(1.0 + 0.18 * jax.random.normal(key_of[15], (C,), jnp.float32), 0.1, 1.9)
    norm2_shift = gaussian(key_of[16], (C,), 0.5, 3.0, (), jnp.float32)
    fc1_weight = gaussian(key_of[17], (C, FFN), C ** -0.5, 0.375)
    fc1_bias = gaussian(key_of[18], (FFN,), 0.5, 3.0, (), jnp.float32)
    fc2_weight = gaussian(key_of[19], (FFN, C), FFN ** -0.5, 0.1875)
    return {"features": features, "neighbours": neighbours, "fetch_table": fetch_table, "hilbert_slot": hilbert_slot, "patch_ids": patch_ids, "conv_weight": conv_weight, "cpe_weight": cpe_weight, "cpe_bias": cpe_bias, "cpe_gain": cpe_gain, "cpe_shift": cpe_shift, "norm1_gain": norm1_gain, "norm1_shift": norm1_shift, "query_weight": query_weight, "pair_weight": pair_weight, "proj_weight": proj_weight, "norm2_gain": norm2_gain, "norm2_shift": norm2_shift, "fc1_weight": fc1_weight, "fc1_bias": fc1_bias, "fc2_weight": fc2_weight}


def layer_norm(values, gain, shift):
    mean = lax.optimization_barrier(jnp.mean(values, axis=-1, keepdims=True))
    centered = values - mean
    var = lax.optimization_barrier(jnp.mean(centered * centered, axis=-1, keepdims=True))
    return centered * lax.rsqrt(var + 1e-05) * gain + shift

def reference(features, neighbours, fetch_table, hilbert_slot, patch_ids, conv_weight, cpe_weight, cpe_bias, cpe_gain, cpe_shift, norm1_gain, norm1_shift, query_weight, pair_weight, proj_weight, norm2_gain, norm2_shift, fc1_weight, fc1_bias, fc2_weight):
    rows_dev = PATCH // N_CHIP
    count = rows_dev // BLOCK
    devices = N_REGION * N_SLAB * N_CHIP
    blocks = features.reshape(N_REGION, N_SLAB, N_CHIP, count, BLOCK, C)
    empty = jnp.zeros_like(blocks[:, :1])
    before = jnp.concatenate([empty, blocks[:, :-1]], axis=1)[:, :, :, count - HALO_B:]
    after = jnp.concatenate([blocks[:, 1:], empty], axis=1)[:, :, :, :HALO_B]
    region_ix = jnp.arange(N_REGION, dtype=jnp.int32).reshape(N_REGION, 1, 1, 1, 1)
    slab_ix = jnp.arange(N_SLAB, dtype=jnp.int32).reshape(1, N_SLAB, 1, 1, 1)
    chip_ix = jnp.arange(N_CHIP, dtype=jnp.int32).reshape(1, 1, N_CHIP, 1, 1)
    global_block = ((region_ix * N_SLAB + slab_ix) * N_CHIP + chip_ix) * count + jnp.maximum(fetch_table, 0)
    fetched = jnp.take(features.reshape(-1, BLOCK, C), global_block.reshape(-1).astype(jnp.int32), axis=0)
    fetched = fetched.reshape(N_REGION, N_SLAB, N_CHIP, N_REGION, FETCH_CAP, BLOCK, C)
    fetched = jnp.where((fetch_table >= 0)[..., None, None], fetched, jnp.zeros_like(fetched))
    fetched = fetched.transpose(3, 1, 2, 0, 4, 5, 6).reshape(devices, N_REGION * FETCH_CAP * BLOCK, C)
    framed = jnp.concatenate([before, blocks, after], axis=3).reshape(devices, (count + 2 * HALO_B) * BLOCK, C)
    pool = jnp.concatenate([framed, fetched], axis=1)
    nbr_dev = neighbours.reshape(OFFSETS, devices, rows_dev).transpose(1, 0, 2)
    kernel = conv_weight.astype(jnp.float32)

    def conv_one(parts):
        pool_d, nbr_d = parts
        valid = nbr_d >= 0
        rows = jnp.take(pool_d, jnp.where(valid, nbr_d, 0), axis=0)
        rows = jnp.where(valid[..., None], rows, jnp.zeros_like(rows))
        return jnp.einsum('kpc,kcd->pd', rows.astype(jnp.float32), kernel).astype(jnp.bfloat16)
    conv = lax.map(conv_one, (pool, nbr_dev)).reshape(-1, C)
    lin = jnp.dot(conv, cpe_weight, preferred_element_type=jnp.float32) + cpe_bias
    x1 = (features.astype(jnp.float32) + layer_norm(lin, cpe_gain, cpe_shift)).astype(jnp.bfloat16)
    x1b = x1.reshape(N_REGION, N_SLAB, N_CHIP, count, BLOCK, C)
    dest_b = hilbert_slot.reshape(N_REGION, N_SLAB, N_CHIP, count)
    target_region = dest_b // count
    target_slot = dest_b % count
    slab_full = jnp.broadcast_to(jnp.arange(N_SLAB, dtype=jnp.int32).reshape(1, N_SLAB, 1, 1), dest_b.shape)
    chip_full = jnp.broadcast_to(jnp.arange(N_CHIP, dtype=jnp.int32).reshape(1, 1, N_CHIP, 1), dest_b.shape)
    placed = jnp.zeros_like(x1b).at[target_region, slab_full, chip_full, target_slot].set(x1b)
    xh = placed.reshape(-1, C)
    h = layer_norm(xh.astype(jnp.float32), norm1_gain, norm1_shift).astype(jnp.bfloat16)
    queries = jnp.dot(h, query_weight, preferred_element_type=jnp.float32).astype(jnp.bfloat16)
    pairs = jnp.dot(h, pair_weight, preferred_element_type=jnp.float32).astype(jnp.bfloat16)
    patches = N_REGION * N_SLAB
    heads = C // HEAD_DIM
    q_p = queries.reshape(patches, PATCH, heads, HEAD_DIM)
    k_p = pairs[:, :C].reshape(patches, PATCH, heads, HEAD_DIM)
    v_p = pairs[:, C:].reshape(patches, PATCH, heads, HEAD_DIM)
    id_p = patch_ids.reshape(patches, PATCH)
    scale = HEAD_DIM ** (-0.5)

    def attend(parts):
        q_h, k_h, v_h, ids = parts
        same = ids[:, None] == ids[None, :]
        scores = jnp.einsum('qhd,khd->hqk', q_h.astype(jnp.float32), k_h.astype(jnp.float32)) * scale
        scores = jnp.where(same[None], scores, jnp.float32(-1e+30))
        top = lax.optimization_barrier(jnp.max(scores, axis=-1, keepdims=True))
        expo = jnp.exp(scores - top)
        weights = (expo / lax.optimization_barrier(jnp.sum(expo, axis=-1, keepdims=True))).astype(jnp.bfloat16)
        return jnp.einsum('hqk,khd->qhd', weights.astype(jnp.float32), v_h.astype(jnp.float32)).astype(jnp.bfloat16)
    att = lax.map(attend, (q_p, k_p, v_p, id_p)).reshape(-1, C)
    x2 = (xh.astype(jnp.float32) + jnp.dot(att, proj_weight, preferred_element_type=jnp.float32)).astype(jnp.bfloat16)
    h2 = layer_norm(x2.astype(jnp.float32), norm2_gain, norm2_shift).astype(jnp.bfloat16)
    hidden = jax.nn.gelu(jnp.dot(h2, fc1_weight, preferred_element_type=jnp.float32) + fc1_bias, approximate=False).astype(jnp.bfloat16)
    return (x2.astype(jnp.float32) + jnp.dot(hidden, fc2_weight, preferred_element_type=jnp.float32)).astype(jnp.bfloat16)
```

```python
import functools

import jax
import jax.numpy as jnp
from jax import lax
from jax.experimental import pallas as pl
from jax.experimental.pallas import tpu as pltpu
from jax.sharding import PartitionSpec as P

HEAD_DIM = 16
BLOCK = 64
HALO_B = 2
LANES = 128
VMEM_BYTES = 48 * 1024 * 1024


def with_halo(block, sides, width):
    for axis, dim in sides:
        count = lax.axis_size(axis)
        forward = [(i, i + 1) for i in range(count - 1)]
        backward = [(target, source) for source, target in forward]
        low = lax.ppermute(
            lax.slice_in_dim(block, block.shape[dim] - width, None, axis=dim), axis, forward
        )
        high = lax.ppermute(lax.slice_in_dim(block, 0, width, axis=dim), axis, backward)
        block = jnp.concatenate([low, block, high], axis=dim)
    return block


def layer_norm(values, gain, shift):
    mean = jnp.mean(values, axis=-1, keepdims=True)
    centered = values - mean
    var = jnp.mean(centered * centered, axis=-1, keepdims=True)
    return centered * lax.rsqrt(var + 1e-05) * gain + shift


def dot32(a, b):
    return jnp.dot(a, b, preferred_element_type=jnp.float32)


def conv_kernel(
    nbr_ref, pool_ref, weight_ref, feat_ref, lin_ref, bias_ref, gain_ref, shift_ref,
    out_ref, codes, marks, acc,
):
    offsets = weight_ref.shape[0]
    rows = feat_ref.shape[0]
    tiles = pool_ref.shape[0] // LANES
    numbers = nbr_ref[...].T
    low = jnp.bitwise_and(numbers, LANES - 1) + LANES
    high = jnp.right_shift(jnp.maximum(numbers, 0), 7)
    coded = jnp.where(numbers >= 0, jnp.left_shift(low, high), 0).astype(jnp.float32)
    for o in range(offsets):
        codes[o] = jnp.broadcast_to(coded[:, o : o + 1], (rows, LANES)).astype(jnp.bfloat16)
    lane = lax.broadcasted_iota(jnp.int32, (16, LANES), 1) + LANES
    for t in range(tiles):
        marks[t] = jnp.left_shift(lane, t).astype(jnp.float32).astype(jnp.bfloat16)
    acc[...] = jnp.zeros_like(acc)
    one = jnp.ones((rows, LANES), jnp.bfloat16)
    zero = jnp.zeros((rows, LANES), jnp.bfloat16)

    def step(o, carry):
        code = codes[o]
        pick = jnp.concatenate(
            [
                jnp.where(code == jnp.tile(marks[t], (rows // 16, 1)), one, zero)
                for t in range(tiles)
            ],
            axis=1,
        )
        got = dot32(pick, pool_ref[...]).astype(jnp.bfloat16)
        acc[...] += dot32(got, weight_ref[o])
        return carry

    lax.fori_loop(0, offsets, step, 0)
    conv = acc[...].astype(jnp.bfloat16)
    lin = dot32(conv, lin_ref[...]) + bias_ref[...]
    out_ref[...] = (
        feat_ref[...].astype(jnp.float32) + layer_norm(lin, gain_ref[...], shift_ref[...])
    ).astype(jnp.bfloat16)


def conv_call(neighbours, pool, weight, features, lin, bias, gain, shift):
    rows, width = features.shape
    offsets = weight.shape[0]
    tiles = pool.shape[0] // LANES
    return pl.pallas_call(
        conv_kernel,
        out_shape=jax.ShapeDtypeStruct((rows, width), jnp.bfloat16),
        in_specs=[pl.BlockSpec(memory_space=pltpu.VMEM)] * 8,
        out_specs=pl.BlockSpec(memory_space=pltpu.VMEM),
        scratch_shapes=[
            pltpu.VMEM((offsets, rows, LANES), jnp.bfloat16),
            pltpu.VMEM((tiles, 16, LANES), jnp.bfloat16),
            pltpu.VMEM((rows, width), jnp.float32),
        ],
        compiler_params=pltpu.CompilerParams(vmem_limit_bytes=VMEM_BYTES),
        name="conv",
    )(neighbours, pool, weight, features, lin, bias[None], gain[None], shift[None])


def tail_kernel(
    rows_ref, query_ref, pairs_ref, own_ref, ids_ref, proj_ref, gain_ref, shift_ref,
    fc1_ref, fc1_bias_ref, fc2_ref, out_ref, bias, mixed, part,
):
    rows, width = rows_ref.shape
    heads = width // HEAD_DIM
    bias[...] = jnp.where(own_ref[...] == ids_ref[...], 0.0, -1e30)
    mixed[...] = jnp.zeros_like(mixed)
    lane = lax.broadcasted_iota(jnp.int32, (1, width), 1) // HEAD_DIM

    def head(h, carry):
        mine = lane == h
        query = jnp.where(mine, query_ref[...], jnp.zeros((), jnp.bfloat16))
        values = jnp.where(mine, pairs_ref[:, width:], jnp.zeros((), jnp.bfloat16))
        keys = pairs_ref[:, :width]
        for r in range(0, rows, part):
            scores = lax.dot_general(
                query[r : r + part], keys, (((1,), (1,)), ((), ())),
                preferred_element_type=jnp.float32,
            ) + bias[r : r + part]
            top = jnp.max(scores, axis=-1, keepdims=True)
            expo = jnp.exp(scores - top)
            total = jnp.sum(expo, axis=-1, keepdims=True)
            weights = (expo * (1.0 / total)).astype(jnp.bfloat16)
            mixed[r : r + part] += dot32(weights, values)
        return carry

    lax.fori_loop(0, heads, head, 0)
    attended = mixed[...].astype(jnp.bfloat16)
    mid = (rows_ref[...].astype(jnp.float32) + dot32(attended, proj_ref[...])).astype(jnp.bfloat16)
    mid32 = mid.astype(jnp.float32)
    normed = layer_norm(mid32, gain_ref[...], shift_ref[...]).astype(jnp.bfloat16)
    pre = dot32(normed, fc1_ref[...]) + fc1_bias_ref[...]
    hidden = (0.5 * pre * (1.0 + lax.erf(pre * (0.5**0.5)))).astype(jnp.bfloat16)
    out_ref[...] = (mid32 + dot32(hidden, fc2_ref[...])).astype(jnp.bfloat16)


def tail_call(reordered, queries, pairs, own_ids, ids, proj, gain, shift, fc1, fc1_bias, fc2):
    rows, width = reordered.shape
    return pl.pallas_call(
        functools.partial(tail_kernel, part=128),
        out_shape=jax.ShapeDtypeStruct((rows, width), jnp.bfloat16),
        in_specs=[pl.BlockSpec(memory_space=pltpu.VMEM)] * 11,
        out_specs=pl.BlockSpec(memory_space=pltpu.VMEM),
        scratch_shapes=[
            pltpu.VMEM((rows, pairs.shape[0]), jnp.float32),
            pltpu.VMEM((rows, width), jnp.float32),
        ],
        compiler_params=pltpu.CompilerParams(vmem_limit_bytes=VMEM_BYTES),
        name="tail",
    )(
        reordered, queries, pairs, own_ids[:, None], ids[None], proj, gain[None], shift[None],
        fc1, fc1_bias[None], fc2,
    )


def local(
    features,
    neighbours,
    fetch_table,
    hilbert_slot,
    patch_ids,
    conv_weight,
    cpe_weight,
    cpe_bias,
    cpe_gain,
    cpe_shift,
    norm1_gain,
    norm1_shift,
    query_weight,
    pair_weight,
    proj_weight,
    norm2_gain,
    norm2_shift,
    fc1_weight,
    fc1_bias,
    fc2_weight,
):
    rows_dev = features.shape[0]
    width = features.shape[1]
    count = rows_dev // BLOCK
    regions = lax.axis_size("region")
    blocks = features.reshape(count, BLOCK, width)
    framed = with_halo(blocks, (("slab", 0),), HALO_B)
    table = fetch_table[:, 0, 0]
    slots = table.shape[2]
    here = lax.axis_index("region")
    outgoing = lax.dynamic_index_in_dim(table, here, 0, keepdims=False)
    chosen = jnp.take(blocks, jnp.maximum(outgoing, 0).reshape(-1), axis=0).reshape(
        regions, slots, BLOCK, width
    )
    chosen = jnp.where((outgoing >= 0)[:, :, None, None], chosen, jnp.zeros_like(chosen))
    fetched = lax.all_to_all(chosen, "region", split_axis=0, concat_axis=0, tiled=True)
    pool = jnp.concatenate([framed.reshape(-1, width), fetched.reshape(-1, width)], axis=0)
    weight = lax.all_gather(conv_weight, "chip", axis=2, tiled=True)
    encoded = conv_call(
        neighbours, pool, weight, features, cpe_weight, cpe_bias, cpe_gain, cpe_shift
    )
    cap = max(1, 2 * count // regions)
    region_of = hilbert_slot // count
    slot_of = hilbert_slot % count
    order = jnp.arange(count, dtype=jnp.int32)
    rank = jnp.sum(
        (region_of[:, None] == region_of[None, :]) & (order[:, None] > order[None, :]), axis=1
    )
    position = region_of * cap + rank
    pick = jnp.arange(regions * cap, dtype=jnp.int32)[:, None] == position[None, :]
    sending = jnp.dot(
        pick.astype(jnp.bfloat16),
        encoded.reshape(count, BLOCK * width),
        preferred_element_type=jnp.float32,
    ).astype(jnp.bfloat16)
    sending = sending.reshape(regions, cap, BLOCK * width)
    labels = (
        (jnp.sum(jnp.where(pick, slot_of[None, :] + 1, 0), axis=1) - 1)
        .astype(jnp.bfloat16)
        .reshape(regions, cap)
    )
    block_numbers = jnp.arange(count, dtype=jnp.int32).astype(jnp.bfloat16)
    arrived, marks = (
        lax.all_to_all(sending, "region", split_axis=0, concat_axis=0, tiled=True),
        lax.all_to_all(labels, "region", split_axis=0, concat_axis=0, tiled=True),
    )
    place_arrived = arrived.reshape(regions * cap, -1)
    place_marks = marks.reshape(-1)
    select = (place_marks[None, :] == block_numbers[:, None]).astype(jnp.bfloat16)
    reordered = (
        jnp.dot(select, place_arrived, preferred_element_type=jnp.float32)
        .astype(jnp.bfloat16)
        .reshape(rows_dev, width)
    )
    normed = layer_norm(reordered.astype(jnp.float32), norm1_gain, norm1_shift).astype(jnp.bfloat16)
    query_rows = jnp.dot(normed, query_weight, preferred_element_type=jnp.float32).astype(
        jnp.bfloat16
    ) * jnp.bfloat16(HEAD_DIM ** (-0.5))
    pair_rows = jnp.dot(normed, pair_weight, preferred_element_type=jnp.float32).astype(
        jnp.bfloat16
    )
    all_pairs = lax.all_gather(pair_rows, "chip", axis=0, tiled=True)
    own_ids = lax.dynamic_slice_in_dim(patch_ids, lax.axis_index("chip") * rows_dev, rows_dev)
    return tail_call(
        reordered, query_rows, all_pairs, own_ids, patch_ids, proj_weight, norm2_gain,
        norm2_shift, fc1_weight, fc1_bias, fc2_weight,
    )


def solution(mesh):
    return jax.shard_map(
        local,
        mesh=mesh,
        in_specs=(
            P(("groups", "region", "slab", "chip"), None),
            P(None, ("groups", "region", "slab", "chip")),
            P("groups", "slab", "chip", None, None),
            P(("groups", "region", "slab", "chip")),
            P(("groups", "region", "slab")),
            P(None, None, "chip"),
            P(),
            P(),
            P(),
            P(),
            P(),
            P(),
            P(),
            P(),
            P(),
            P(),
            P(),
            P(),
            P(),
            P(),
        ),
        out_specs=P(("groups", "region", "slab", "chip"), None),
        check_vma=False,
    )
```

```python
import functools

import jax
import jax.numpy as jnp
from jax import lax
from jax.experimental import pallas as pl
from jax.experimental.pallas import tpu as pltpu
from jax.sharding import PartitionSpec as P

HEAD_DIM = 16
BLOCK = 64
HALO_B = 2
LANES = 128
VMEM_BYTES = 48 * 1024 * 1024


def layer_norm(values, gain, shift):
    mean = jnp.mean(values, axis=-1, keepdims=True)
    centered = values - mean
    var = jnp.mean(centered * centered, axis=-1, keepdims=True)
    return centered * lax.rsqrt(var + 1e-05) * gain + shift


def dot32(a, b):
    return jnp.dot(a, b, preferred_element_type=jnp.float32)


def front_kernel(
    sizes, table_ref, slot_ref, half_ref, *refs,
):
    sources_hbm, (rows_ref, query_ref, pairs_ref) = refs[:10], refs[10:13]
    (
        codes, marks, acc, held, rest, weight, fetch_out, label_out, label_in, moved_out,
        moved_in, pairs_in, fetch_sem, halo_sem, weight_sem, label_sem, moved_sem, pairs_sem,
        local_sem, load_sem,
    ) = refs[13:33]
    loads = [
        pltpu.make_async_copy(source, held_here, load_sem.at[i])
        for i, (source, held_here) in enumerate(zip(sources_hbm, refs[33:]))
    ]
    for load in loads:
        load.start()
    (
        feat_ref, nbr_ref, lin_ref, bias_ref, gain_ref, shift_ref, gain1_ref, shift1_ref, wq_ref,
        wp_ref,
    ) = refs[33:]
    regions, slabs, chips, slots, cap = sizes
    offsets = weight.shape[0]
    rows, width = feat_ref.shape
    count = rows // BLOCK
    halo = HALO_B * BLOCK
    own_tiles = rows // LANES
    rest_tiles = rest.shape[0] // LANES
    halo_tiles = halo // LANES
    together = 3 if offsets % 3 == 0 else 1
    here, slab, chip = lax.axis_index("region"), lax.axis_index("slab"), lax.axis_index("chip")
    right, left = lax.rem(slab + 1, slabs), lax.rem(slab + slabs - 1, slabs)
    peers = [{"region": lax.rem(here + d, regions)} for d in range(1, regions)]
    mate = {"chip": 1 - chip}

    barrier = pltpu.get_barrier_semaphore()
    for device in peers + [{"slab": right}, {"slab": left}, mate]:
        pl.semaphore_signal(
            barrier, inc=1, device_id=device, device_id_type=pl.DeviceIdType.MESH
        )
    pl.semaphore_wait(barrier, len(peers) + 3)

    def send(src, dst, sems, at, device):
        copy = pltpu.make_async_remote_copy(
            src_ref=src, dst_ref=dst, send_sem=sems.at[0, at], recv_sem=sems.at[1, at],
            device_id=device, device_id_type=pl.DeviceIdType.MESH,
        )
        copy.start()
        return copy

    mine = weight.at[:, :, pl.ds(pl.multiple_of(chip * half_ref.shape[2], LANES), half_ref.shape[2])]
    weight_copy = send(half_ref, mine, weight_sem, 0, mate)
    weight_own = pltpu.make_async_copy(half_ref, mine, local_sem)
    weight_own.start()

    loads[0].wait()

    def chosen(number, ref):
        label = jnp.full((1, width), number.astype(jnp.float32)).astype(jnp.bfloat16)
        block = jnp.zeros((BLOCK, width), jnp.bfloat16)
        for b in range(count):
            block = jnp.where(
                label == jnp.bfloat16(b), ref[b * BLOCK : (b + 1) * BLOCK, :], block
            )
        return block

    fetches = []
    for d in range(regions):
        to = lax.rem(here + d, regions)
        for k in range(slots):
            block = chosen(table_ref[(here * regions + to) * slots + k], feat_ref)
            if d == 0:
                at = 2 * halo + (here * slots + k) * BLOCK
                rest[pl.ds(pl.multiple_of(at, BLOCK), BLOCK), :] = block
            else:
                fetch_out[d - 1, k * BLOCK : (k + 1) * BLOCK, :] = block
        if d > 0:
            at = pl.multiple_of(2 * halo + here * slots * BLOCK, slots * BLOCK)
            fetches.append(
                send(
                    fetch_out.at[d - 1], rest.at[pl.ds(at, slots * BLOCK)], fetch_sem, d - 1,
                    peers[d - 1],
                )
            )
    low = send(
        feat_ref.at[pl.ds(rows - halo, halo)], rest.at[pl.ds(0, halo)], halo_sem, 0,
        {"slab": right},
    )
    high = send(
        feat_ref.at[pl.ds(0, halo)], rest.at[pl.ds(halo, halo)], halo_sem, 1, {"slab": left}
    )

    placed = [slot_ref[b] for b in range(count)]
    region_of = [lax.div(p, count) for p in placed]
    rank = [
        sum([jnp.where(region_of[a] == region_of[b], 1, 0) for a in range(b)], jnp.int32(0))
        for b in range(count)
    ]
    sources = []
    line = lax.broadcasted_iota(jnp.int32, (16, LANES), 0)
    labels = []
    for d in range(regions):
        to = lax.rem(here + d, regions)
        text = jnp.full((16, LANES), -1, jnp.int32)
        source = []
        for k in range(cap):
            block, label = jnp.int32(0), jnp.int32(-1)
            for b in range(count):
                hit = jnp.logical_and(region_of[b] == to, rank[b] == k)
                block = jnp.where(hit, b, block)
                label = jnp.where(hit, lax.rem(placed[b], count), label)
            source.append(block)
            text = jnp.where(line == k, label, text)
        sources.append(source)
        text = text.astype(jnp.float32).astype(jnp.bfloat16)
        if d == 0:
            label_in[0] = text
        else:
            label_out[d - 1] = text
            labels.append(send(label_out.at[d - 1], label_in.at[d], label_sem, d - 1, peers[d - 1]))

    loads[1].wait()
    numbers = nbr_ref[...].T
    low_part = jnp.bitwise_and(numbers, LANES - 1) + LANES
    high_part = jnp.right_shift(jnp.maximum(numbers, 0), 7)
    coded = jnp.where(numbers >= 0, jnp.left_shift(low_part, high_part), 0).astype(jnp.float32)
    for o in range(offsets):
        codes[o] = jnp.broadcast_to(coded[:, o : o + 1], (rows, LANES)).astype(jnp.bfloat16)
    lane = lax.broadcasted_iota(jnp.int32, (16, LANES), 1) + LANES
    for t in range(own_tiles + rest_tiles):
        marks[t] = jnp.left_shift(lane, t).astype(jnp.float32).astype(jnp.bfloat16)
    one = jnp.ones((rows, LANES), jnp.bfloat16)
    zero = jnp.zeros((rows, LANES), jnp.bfloat16)

    def picks(i, tiles):
        lines = []
        for j in range(together):
            code = codes[i * together + j]
            lines.append(
                jnp.concatenate(
                    [
                        jnp.where(code == jnp.tile(marks[t], (rows // 16, 1)), one, zero)
                        for t in tiles
                    ],
                    axis=1,
                )
            )
        return jnp.concatenate(lines, axis=0)

    def own_step(i, carry):
        pick = picks(i, range(halo_tiles, halo_tiles + own_tiles))
        held[i] = dot32(pick, feat_ref[...]).astype(jnp.bfloat16)
        return carry

    lax.fori_loop(0, offsets // together, own_step, 0)
    acc[...] = jnp.zeros_like(acc)
    for copy in fetches + [low, high, weight_copy] + loads[2:]:
        copy.wait()
    weight_own.wait()
    first = rest[0:halo, :]
    rest[0:halo, :] = jnp.where(slab > 0, first, jnp.zeros_like(first))
    second = rest[halo : 2 * halo, :]
    rest[halo : 2 * halo, :] = jnp.where(slab < slabs - 1, second, jnp.zeros_like(second))
    others = list(range(halo_tiles)) + list(
        range(halo_tiles + own_tiles, own_tiles + rest_tiles)
    )

    def rest_step(i, carry):
        got = dot32(picks(i, others), rest[...]).astype(jnp.bfloat16) + held[i]
        total = acc[...]
        for j in range(together):
            total += dot32(got[j * rows : (j + 1) * rows], weight[i * together + j])
        acc[...] = total
        return carry

    lax.fori_loop(0, offsets // together, rest_step, 0)
    conv = acc[...].astype(jnp.bfloat16)
    lin = dot32(conv, lin_ref[...]) + bias_ref[...]
    rows_ref[...] = (
        feat_ref[...].astype(jnp.float32) + layer_norm(lin, gain_ref[...], shift_ref[...])
    ).astype(jnp.bfloat16)

    moves = []
    for d in list(range(1, regions)) + [0]:
        for k in range(cap):
            block = chosen(sources[d][k], rows_ref)
            if d == 0:
                moved_in[0, k * BLOCK : (k + 1) * BLOCK, :] = block
            else:
                moved_out[d - 1, k * BLOCK : (k + 1) * BLOCK, :] = block
        if d > 0:
            moves.append(send(moved_out.at[d - 1], moved_in.at[d], moved_sem, d - 1, peers[d - 1]))
    for copy in labels + moves:
        copy.wait()
    for j in range(count):
        block = jnp.zeros((BLOCK, width), jnp.bfloat16)
        for d in range(regions):
            for k in range(cap):
                label = jnp.tile(label_in[d, k : k + 1, :], (1, width // LANES))
                block = jnp.where(
                    label == jnp.bfloat16(j), moved_in[d, k * BLOCK : (k + 1) * BLOCK, :], block
                )
        rows_ref[j * BLOCK : (j + 1) * BLOCK, :] = block

    normed = layer_norm(
        rows_ref[...].astype(jnp.float32), gain1_ref[...], shift1_ref[...]
    ).astype(jnp.bfloat16)
    ours = pl.ds(pl.multiple_of(chip * rows, rows), rows)
    theirs = pl.ds(pl.multiple_of((1 - chip) * rows, rows), rows)
    pairs = dot32(normed, wp_ref[...]).astype(jnp.bfloat16)
    pairs_in[ours, :] = pairs
    pairs_copy = send(pairs_in.at[ours], pairs_in.at[ours], pairs_sem, 0, mate)
    pairs_ref[ours, :] = pairs
    query = dot32(normed, wq_ref[...]).astype(jnp.bfloat16)
    query_ref[...] = query * jnp.bfloat16(HEAD_DIM ** (-0.5))
    pairs_copy.wait()
    pairs_ref[theirs, :] = pairs_in[theirs, :]


def front_call(
    table, hilbert_slot, neighbours, features, half, lin, bias, gain, shift, gain1, shift1, wq, wp
):
    rows, width = features.shape
    offsets = half.shape[0]
    regions, slabs, chips = (lax.axis_size(axis) for axis in ("region", "slab", "chip"))
    slots = table.shape[2]
    count = rows // BLOCK
    cap = max(1, 2 * count // regions)
    together = 3 if offsets % 3 == 0 else 1
    rest_rows = (2 * HALO_B + regions * slots) * BLOCK
    tiles = (rows + rest_rows) // LANES
    vmem = pl.BlockSpec(memory_space=pltpu.VMEM)
    smem = pl.BlockSpec(memory_space=pltpu.SMEM)
    loaded = [
        features, neighbours, lin, bias[None], gain[None], shift[None], gain1[None],
        shift1[None], wq, wp,
    ]
    shape = jax.ShapeDtypeStruct
    return pl.pallas_call(
        functools.partial(front_kernel, (regions, slabs, chips, slots, cap)),
        out_shape=[
            shape((rows, width), jnp.bfloat16),
            shape((rows, width), jnp.bfloat16),
            shape((chips * rows, 2 * width), jnp.bfloat16),
        ],
        in_specs=[smem, smem] + [pl.BlockSpec(memory_space=pl.ANY)] * (1 + len(loaded)),
        out_specs=[vmem] * 3,
        scratch_shapes=[
            pltpu.VMEM((offsets, rows, LANES), jnp.bfloat16),
            pltpu.VMEM((tiles, 16, LANES), jnp.bfloat16),
            pltpu.VMEM((rows, width), jnp.float32),
            pltpu.VMEM((offsets // together, together * rows, width), jnp.bfloat16),
            pltpu.VMEM((rest_rows, width), jnp.bfloat16),
            pltpu.VMEM((offsets, width, chips * half.shape[2]), jnp.bfloat16),
            pltpu.VMEM((regions - 1, slots * BLOCK, width), jnp.bfloat16),
            pltpu.VMEM((regions - 1, 16, LANES), jnp.bfloat16),
            pltpu.VMEM((regions, 16, LANES), jnp.bfloat16),
            pltpu.VMEM((regions - 1, cap * BLOCK, width), jnp.bfloat16),
            pltpu.VMEM((regions, cap * BLOCK, width), jnp.bfloat16),
            pltpu.VMEM((chips * rows, 2 * width), jnp.bfloat16),
            pltpu.SemaphoreType.DMA((2, regions - 1)),
            pltpu.SemaphoreType.DMA((2, 2)),
            pltpu.SemaphoreType.DMA((2, 1)),
            pltpu.SemaphoreType.DMA((2, regions - 1)),
            pltpu.SemaphoreType.DMA((2, regions - 1)),
            pltpu.SemaphoreType.DMA((2, 1)),
            pltpu.SemaphoreType.DMA,
            pltpu.SemaphoreType.DMA((len(loaded),)),
        ]
        + [pltpu.VMEM(array.shape, array.dtype) for array in loaded],
        compiler_params=pltpu.CompilerParams(
            vmem_limit_bytes=VMEM_BYTES, collective_id=0, has_side_effects=True
        ),
        name="front",
    )(table.reshape(-1), hilbert_slot, half, *loaded)


def tail_kernel(
    rows_ref, query_ref, pairs_ref, ids_ref, proj_ref, gain_ref, shift_ref,
    fc1_ref, fc1_bias_ref, fc2_ref, out_ref, ids, key_marks, own_marks, values, even, odd, mixed,
):
    rows, width = rows_ref.shape
    count = pairs_ref.shape[0]
    heads = width // HEAD_DIM
    zero = jnp.zeros((), jnp.bfloat16)
    lane = lax.broadcasted_iota(jnp.int32, (1, width), 1)
    scan = jnp.bitwise_and(lane, LANES - 1)
    ids[...] = jnp.broadcast_to(ids_ref[...], (LANES, count)).T
    column = jnp.tile(ids[...], (1, width // LANES))
    key_marks[...] = jnp.where(column == scan, 1.0, 0.0).astype(jnp.bfloat16)
    start = pl.multiple_of(lax.axis_index("chip") * rows, rows)
    own = jnp.tile(ids[pl.ds(start, rows), :], (1, width // LANES))
    own_marks[...] = jnp.where(own == scan, 0.0, -1e30).astype(jnp.bfloat16)
    values[...] = pairs_ref[:, width:].T

    def score(h, out):
        mine = lane // HEAD_DIM == h
        query = jnp.where(mine, query_ref[...], own_marks[...])
        keys = jnp.where(mine, pairs_ref[:, :width], key_marks[...])
        out[...] = lax.dot_general(
            keys, query, (((1,), (1,)), ((), ())), preferred_element_type=jnp.float32
        )

    def attend(h, scores):
        held = scores[...]
        top = jnp.max(held, axis=0, keepdims=True)
        expo = jnp.exp(held - top)
        total = jnp.sum(expo, axis=0, keepdims=True)
        weights = (expo * (1.0 / total)).astype(jnp.bfloat16)
        at = pl.ds(pl.multiple_of(h * HEAD_DIM, HEAD_DIM), HEAD_DIM)
        mixed[at, :] = dot32(values[at, :], weights).astype(jnp.bfloat16)

    score(0, even)

    def two_heads(i, carry):
        h = 2 * i
        score(h + 1, odd)
        attend(h, even)
        score(jnp.minimum(h + 2, heads - 1), even)
        attend(h + 1, odd)
        return carry

    lax.fori_loop(0, heads // 2, two_heads, 0)
    attended = mixed[...].T
    mid = (rows_ref[...].astype(jnp.float32) + dot32(attended, proj_ref[...])).astype(jnp.bfloat16)
    mid32 = mid.astype(jnp.float32)
    normed = layer_norm(mid32, gain_ref[...], shift_ref[...]).astype(jnp.bfloat16)
    pre = dot32(normed, fc1_ref[...]) + fc1_bias_ref[...]
    hidden = (0.5 * pre * (1.0 + lax.erf(pre * (0.5**0.5)))).astype(jnp.bfloat16)
    out_ref[...] = (mid32 + dot32(hidden, fc2_ref[...])).astype(jnp.bfloat16)


def tail_call(reordered, queries, pairs, ids, proj, gain, shift, fc1, fc1_bias, fc2):
    rows, width = reordered.shape
    count = pairs.shape[0]
    return pl.pallas_call(
        tail_kernel,
        out_shape=jax.ShapeDtypeStruct((rows, width), jnp.bfloat16),
        in_specs=[pl.BlockSpec(memory_space=pltpu.VMEM)] * 10,
        out_specs=pl.BlockSpec(memory_space=pltpu.VMEM),
        scratch_shapes=[
            pltpu.VMEM((count, LANES), jnp.int32),
            pltpu.VMEM((count, width), jnp.bfloat16),
            pltpu.VMEM((rows, width), jnp.bfloat16),
            pltpu.VMEM((width, count), jnp.bfloat16),
            pltpu.VMEM((count, rows), jnp.float32),
            pltpu.VMEM((count, rows), jnp.float32),
            pltpu.VMEM((width, rows), jnp.bfloat16),
        ],
        compiler_params=pltpu.CompilerParams(vmem_limit_bytes=VMEM_BYTES),
        name="tail",
    )(
        reordered, queries, pairs, ids[None], proj, gain[None], shift[None],
        fc1, fc1_bias[None], fc2,
    )


def local(
    features,
    neighbours,
    fetch_table,
    hilbert_slot,
    patch_ids,
    conv_weight,
    cpe_weight,
    cpe_bias,
    cpe_gain,
    cpe_shift,
    norm1_gain,
    norm1_shift,
    query_weight,
    pair_weight,
    proj_weight,
    norm2_gain,
    norm2_shift,
    fc1_weight,
    fc1_bias,
    fc2_weight,
):
    rows_dev = features.shape[0]
    reordered, query_rows, all_pairs = front_call(
        fetch_table[:, 0, 0], hilbert_slot, neighbours, features, conv_weight, cpe_weight,
        cpe_bias, cpe_gain, cpe_shift, norm1_gain, norm1_shift, query_weight, pair_weight,
    )
    return tail_call(
        reordered, query_rows, all_pairs, patch_ids, proj_weight, norm2_gain,
        norm2_shift, fc1_weight, fc1_bias, fc2_weight,
    )


def solution(mesh):
    return jax.shard_map(
        local,
        mesh=mesh,
        in_specs=(
            P(("groups", "region", "slab", "chip"), None),
            P(None, ("groups", "region", "slab", "chip")),
            P("groups", "slab", "chip", None, None),
            P(("groups", "region", "slab", "chip")),
            P(("groups", "region", "slab")),
            P(None, None, "chip"),
            P(),
            P(),
            P(),
            P(),
            P(),
            P(),
            P(),
            P(),
            P(),
            P(),
            P(),
            P(),
            P(),
            P(),
        ),
        out_specs=P(("groups", "region", "slab", "chip"), None),
        check_vma=False,
    )
```

```python
import functools

import jax
import jax.numpy as jnp
from jax import lax
from jax.experimental import pallas as pl
from jax.experimental.pallas import tpu as pltpu
from jax.sharding import PartitionSpec as P

HEAD_DIM = 16
BLOCK = 64
HALO_B = 2
LANES = 128
VMEM_BYTES = 64 * 1024 * 1024


def layer_norm(values, gain, shift):
    mean = jnp.mean(values, axis=-1, keepdims=True)
    centered = values - mean
    var = jnp.mean(centered * centered, axis=-1, keepdims=True)
    return centered * lax.rsqrt(var + 1e-05) * gain + shift


def dot32(a, b):
    return jnp.dot(a, b, preferred_element_type=jnp.float32)


def front_kernel(
    sizes, table_ref, slot_ref, half_ref, *refs,
):
    sources_hbm, results = refs[:10], refs[10:13]
    (
        codes, marks, acc, held, rest, weight, fetch_out, label_out, label_in, moved_out,
        moved_in, pairs_in, fetch_sem, halo_sem, weight_sem, label_sem, moved_sem, pairs_sem,
        local_sem, load_sem, rows_ref, query_ref, pairs_ref, save_sem,
    ) = refs[13:37]
    loads = [
        pltpu.make_async_copy(source, held_here, load_sem.at[i])
        for i, (source, held_here) in enumerate(zip(sources_hbm, refs[37:]))
    ]
    for load in loads:
        load.start()
    (
        feat_ref, nbr_ref, lin_ref, bias_ref, gain_ref, shift_ref, gain1_ref, shift1_ref, wq_ref,
        wp_ref,
    ) = refs[37:]
    regions, slabs, chips, slots, cap = sizes
    offsets = weight.shape[0]
    rows, width = feat_ref.shape
    count = rows // BLOCK
    halo = HALO_B * BLOCK
    own_tiles = rows // LANES
    rest_tiles = rest.shape[0] // LANES
    halo_tiles = halo // LANES
    together = 3 if offsets % 3 == 0 else 1
    here, slab, chip = lax.axis_index("region"), lax.axis_index("slab"), lax.axis_index("chip")
    right, left = lax.rem(slab + 1, slabs), lax.rem(slab + slabs - 1, slabs)
    peers = [{"region": lax.rem(here + d, regions)} for d in range(1, regions)]
    mate = {"chip": 1 - chip}

    barrier = pltpu.get_barrier_semaphore()
    for device in peers + [{"slab": right}, {"slab": left}, mate]:
        pl.semaphore_signal(
            barrier, inc=1, device_id=device, device_id_type=pl.DeviceIdType.MESH
        )
    pl.semaphore_wait(barrier, len(peers) + 3)

    def send(src, dst, sems, at, device):
        copy = pltpu.make_async_remote_copy(
            src_ref=src, dst_ref=dst, send_sem=sems.at[0, at], recv_sem=sems.at[1, at],
            device_id=device, device_id_type=pl.DeviceIdType.MESH,
        )
        copy.start()
        return copy

    mine = weight.at[:, :, pl.ds(pl.multiple_of(chip * half_ref.shape[2], LANES), half_ref.shape[2])]
    weight_copy = send(half_ref, mine, weight_sem, 0, mate)
    weight_own = pltpu.make_async_copy(half_ref, mine, local_sem)
    weight_own.start()

    loads[0].wait()

    def chosen(number, ref):
        label = jnp.full((1, width), number.astype(jnp.float32)).astype(jnp.bfloat16)
        block = jnp.zeros((BLOCK, width), jnp.bfloat16)
        for b in range(count):
            block = jnp.where(
                label == jnp.bfloat16(b), ref[b * BLOCK : (b + 1) * BLOCK, :], block
            )
        return block

    fetches = []
    for d in range(regions):
        to = lax.rem(here + d, regions)
        for k in range(slots):
            block = chosen(table_ref[here, 0, 0, to, k], feat_ref)
            if d == 0:
                at = 2 * halo + (here * slots + k) * BLOCK
                rest[pl.ds(pl.multiple_of(at, BLOCK), BLOCK), :] = block
            else:
                fetch_out[d - 1, k * BLOCK : (k + 1) * BLOCK, :] = block
        if d > 0:
            at = pl.multiple_of(2 * halo + here * slots * BLOCK, slots * BLOCK)
            fetches.append(
                send(
                    fetch_out.at[d - 1], rest.at[pl.ds(at, slots * BLOCK)], fetch_sem, d - 1,
                    peers[d - 1],
                )
            )
    low = send(
        feat_ref.at[pl.ds(rows - halo, halo)], rest.at[pl.ds(0, halo)], halo_sem, 0,
        {"slab": right},
    )
    high = send(
        feat_ref.at[pl.ds(0, halo)], rest.at[pl.ds(halo, halo)], halo_sem, 1, {"slab": left}
    )

    placed = [slot_ref[b] for b in range(count)]
    region_of = [lax.div(p, count) for p in placed]
    rank = [
        sum([jnp.where(region_of[a] == region_of[b], 1, 0) for a in range(b)], jnp.int32(0))
        for b in range(count)
    ]
    sources = []
    line = lax.broadcasted_iota(jnp.int32, (16, LANES), 0)
    labels = []
    for d in range(regions):
        to = lax.rem(here + d, regions)
        text = jnp.full((16, LANES), -1, jnp.int32)
        source = []
        for k in range(cap):
            block, label = jnp.int32(0), jnp.int32(-1)
            for b in range(count):
                hit = jnp.logical_and(region_of[b] == to, rank[b] == k)
                block = jnp.where(hit, b, block)
                label = jnp.where(hit, lax.rem(placed[b], count), label)
            source.append(block)
            text = jnp.where(line == k, label, text)
        sources.append(source)
        text = text.astype(jnp.float32).astype(jnp.bfloat16)
        if d == 0:
            label_in[0] = text
        else:
            label_out[d - 1] = text
            labels.append(send(label_out.at[d - 1], label_in.at[d], label_sem, d - 1, peers[d - 1]))

    loads[1].wait()
    numbers = nbr_ref[...].T
    low_part = jnp.bitwise_and(numbers, LANES - 1) + LANES
    high_part = jnp.right_shift(jnp.maximum(numbers, 0), 7)
    coded = jnp.where(numbers >= 0, jnp.left_shift(low_part, high_part), 0).astype(jnp.float32)
    for o in range(offsets):
        codes[o] = jnp.broadcast_to(coded[:, o : o + 1], (rows, LANES)).astype(jnp.bfloat16)
    lane = lax.broadcasted_iota(jnp.int32, (16, LANES), 1) + LANES
    for t in range(own_tiles + rest_tiles):
        marks[t] = jnp.left_shift(lane, t).astype(jnp.float32).astype(jnp.bfloat16)
    one = jnp.ones((rows, LANES), jnp.bfloat16)
    zero = jnp.zeros((rows, LANES), jnp.bfloat16)

    def picks(i, tiles):
        lines = []
        for j in range(together):
            code = codes[i * together + j]
            lines.append(
                jnp.concatenate(
                    [
                        jnp.where(code == jnp.tile(marks[t], (rows // 16, 1)), one, zero)
                        for t in tiles
                    ],
                    axis=1,
                )
            )
        return jnp.concatenate(lines, axis=0)

    def own_step(i, carry):
        pick = picks(i, range(halo_tiles, halo_tiles + own_tiles))
        held[i] = dot32(pick, feat_ref[...]).astype(jnp.bfloat16)
        return carry

    lax.fori_loop(0, offsets // together, own_step, 0)
    acc[...] = jnp.zeros_like(acc)
    for copy in fetches + [low, high, weight_copy] + loads[2:]:
        copy.wait()
    weight_own.wait()
    first = rest[0:halo, :]
    rest[0:halo, :] = jnp.where(slab > 0, first, jnp.zeros_like(first))
    second = rest[halo : 2 * halo, :]
    rest[halo : 2 * halo, :] = jnp.where(slab < slabs - 1, second, jnp.zeros_like(second))
    others = list(range(halo_tiles)) + list(
        range(halo_tiles + own_tiles, own_tiles + rest_tiles)
    )

    def rest_step(i, carry):
        got = dot32(picks(i, others), rest[...]).astype(jnp.bfloat16) + held[i]
        total = acc[...]
        for j in range(together):
            total += dot32(got[j * rows : (j + 1) * rows], weight[i * together + j])
        acc[...] = total
        return carry

    lax.fori_loop(0, offsets // together, rest_step, 0)
    conv = acc[...].astype(jnp.bfloat16)
    lin = dot32(conv, lin_ref[...]) + bias_ref[...]
    rows_ref[...] = (
        feat_ref[...].astype(jnp.float32) + layer_norm(lin, gain_ref[...], shift_ref[...])
    ).astype(jnp.bfloat16)

    moves = []
    for d in list(range(1, regions)) + [0]:
        for k in range(cap):
            block = chosen(sources[d][k], rows_ref)
            if d == 0:
                moved_in[0, k * BLOCK : (k + 1) * BLOCK, :] = block
            else:
                moved_out[d - 1, k * BLOCK : (k + 1) * BLOCK, :] = block
        if d > 0:
            moves.append(send(moved_out.at[d - 1], moved_in.at[d], moved_sem, d - 1, peers[d - 1]))
    for copy in labels + moves:
        copy.wait()
    for j in range(count):
        block = jnp.zeros((BLOCK, width), jnp.bfloat16)
        for d in range(regions):
            for k in range(cap):
                label = jnp.tile(label_in[d, k : k + 1, :], (1, width // LANES))
                block = jnp.where(
                    label == jnp.bfloat16(j), moved_in[d, k * BLOCK : (k + 1) * BLOCK, :], block
                )
        rows_ref[j * BLOCK : (j + 1) * BLOCK, :] = block

    normed = layer_norm(
        rows_ref[...].astype(jnp.float32), gain1_ref[...], shift1_ref[...]
    ).astype(jnp.bfloat16)
    ours = pl.ds(pl.multiple_of(chip * rows, rows), rows)
    theirs = pl.ds(pl.multiple_of((1 - chip) * rows, rows), rows)
    pairs = dot32(normed, wp_ref[...]).astype(jnp.bfloat16)
    pairs_in[ours, :] = pairs
    pairs_copy = send(pairs_in.at[ours], pairs_in.at[ours], pairs_sem, 0, mate)
    pairs_ref[ours, :] = pairs
    query = dot32(normed, wq_ref[...]).astype(jnp.bfloat16)
    query_ref[...] = query * jnp.bfloat16(HEAD_DIM ** (-0.5))
    saves = [
        pltpu.make_async_copy(rows_ref, results[0], save_sem.at[0]),
        pltpu.make_async_copy(query_ref, results[1], save_sem.at[1]),
        pltpu.make_async_copy(pairs_ref.at[ours], results[2].at[ours], save_sem.at[2]),
    ]
    for save in saves:
        save.start()
    pairs_copy.wait()
    saves.append(
        pltpu.make_async_copy(pairs_in.at[theirs], results[2].at[theirs], save_sem.at[3])
    )
    saves[3].start()
    for save in saves:
        save.wait()


def front_call(
    table, hilbert_slot, neighbours, features, half, lin, bias, gain, shift, gain1, shift1, wq, wp
):
    rows, width = features.shape
    offsets = half.shape[0]
    regions, slabs, chips = (lax.axis_size(axis) for axis in ("region", "slab", "chip"))
    slots = table.shape[4]
    count = rows // BLOCK
    cap = max(1, 2 * count // regions)
    together = 3 if offsets % 3 == 0 else 1
    rest_rows = (2 * HALO_B + regions * slots) * BLOCK
    tiles = (rows + rest_rows) // LANES
    smem = pl.BlockSpec(memory_space=pltpu.SMEM)
    loaded = [
        features, neighbours, lin, bias[None], gain[None], shift[None], gain1[None],
        shift1[None], wq, wp,
    ]
    shape = jax.ShapeDtypeStruct
    return pl.pallas_call(
        functools.partial(front_kernel, (regions, slabs, chips, slots, cap)),
        out_shape=[
            shape((rows, width), jnp.bfloat16),
            shape((rows, width), jnp.bfloat16),
            shape((chips * rows, 2 * width), jnp.bfloat16),
        ],
        in_specs=[smem, smem] + [pl.BlockSpec(memory_space=pltpu.HBM)] * (1 + len(loaded)),
        out_specs=[pl.BlockSpec(memory_space=pltpu.HBM)] * 3,
        scratch_shapes=[
            pltpu.VMEM((offsets, rows, LANES), jnp.bfloat16),
            pltpu.VMEM((tiles, 16, LANES), jnp.bfloat16),
            pltpu.VMEM((rows, width), jnp.float32),
            pltpu.VMEM((offsets // together, together * rows, width), jnp.bfloat16),
            pltpu.VMEM((rest_rows, width), jnp.bfloat16),
            pltpu.VMEM((offsets, width, chips * half.shape[2]), jnp.bfloat16),
            pltpu.VMEM((regions - 1, slots * BLOCK, width), jnp.bfloat16),
            pltpu.VMEM((regions - 1, 16, LANES), jnp.bfloat16),
            pltpu.VMEM((regions, 16, LANES), jnp.bfloat16),
            pltpu.VMEM((regions - 1, cap * BLOCK, width), jnp.bfloat16),
            pltpu.VMEM((regions, cap * BLOCK, width), jnp.bfloat16),
            pltpu.VMEM((chips * rows, 2 * width), jnp.bfloat16),
            pltpu.SemaphoreType.DMA((2, regions - 1)),
            pltpu.SemaphoreType.DMA((2, 2)),
            pltpu.SemaphoreType.DMA((2, 1)),
            pltpu.SemaphoreType.DMA((2, regions - 1)),
            pltpu.SemaphoreType.DMA((2, regions - 1)),
            pltpu.SemaphoreType.DMA((2, 1)),
            pltpu.SemaphoreType.DMA,
            pltpu.SemaphoreType.DMA((len(loaded),)),
            pltpu.VMEM((rows, width), jnp.bfloat16),
            pltpu.VMEM((rows, width), jnp.bfloat16),
            pltpu.VMEM((chips * rows, 2 * width), jnp.bfloat16),
            pltpu.SemaphoreType.DMA((4,)),
        ]
        + [pltpu.VMEM(array.shape, array.dtype) for array in loaded],
        compiler_params=pltpu.CompilerParams(
            vmem_limit_bytes=VMEM_BYTES, collective_id=0, has_side_effects=True
        ),
        name="front",
    )(table, hilbert_slot, half, *loaded)


def tail_kernel(
    *refs,
):
    out_ref, ids, key_marks, own_marks, values, even, odd, mixed, load_sem = refs[10:19]
    loads = [
        pltpu.make_async_copy(source, held, load_sem.at[i])
        for i, (source, held) in enumerate(zip(refs[:10], refs[19:]))
    ]
    for load in loads:
        load.start()
    (
        pairs_ref, query_ref, ids_ref, rows_ref, proj_ref, gain_ref, shift_ref, fc1_ref,
        fc1_bias_ref, fc2_ref,
    ) = refs[19:]
    for load in loads[:3]:
        load.wait()
    rows, width = rows_ref.shape
    count = pairs_ref.shape[0]
    heads = width // HEAD_DIM
    zero = jnp.zeros((), jnp.bfloat16)
    lane = lax.broadcasted_iota(jnp.int32, (1, width), 1)
    scan = jnp.bitwise_and(lane, LANES - 1)
    ids[...] = jnp.broadcast_to(ids_ref[...], (LANES, count)).T
    column = jnp.tile(ids[...], (1, width // LANES))
    key_marks[...] = jnp.where(column == scan, 1.0, 0.0).astype(jnp.bfloat16)
    start = pl.multiple_of(lax.axis_index("chip") * rows, rows)
    own = jnp.tile(ids[pl.ds(start, rows), :], (1, width // LANES))
    own_marks[...] = jnp.where(own == scan, 0.0, -1e30).astype(jnp.bfloat16)
    values[...] = pairs_ref[:, width:].T

    def score(h, out):
        mine = lane // HEAD_DIM == h
        query = jnp.where(mine, query_ref[...], own_marks[...])
        keys = jnp.where(mine, pairs_ref[:, :width], key_marks[...])
        out[...] = lax.dot_general(
            keys, query, (((1,), (1,)), ((), ())), preferred_element_type=jnp.float32
        )

    def attend(h, scores):
        held = scores[...]
        top = jnp.max(held, axis=0, keepdims=True)
        expo = jnp.exp(held - top)
        total = jnp.sum(expo, axis=0, keepdims=True)
        weights = (expo * (1.0 / total)).astype(jnp.bfloat16)
        at = pl.ds(pl.multiple_of(h * HEAD_DIM, HEAD_DIM), HEAD_DIM)
        mixed[at, :] = dot32(values[at, :], weights).astype(jnp.bfloat16)

    score(0, even)

    def two_heads(i, carry):
        h = 2 * i
        score(h + 1, odd)
        attend(h, even)
        score(jnp.minimum(h + 2, heads - 1), even)
        attend(h + 1, odd)
        return carry

    lax.fori_loop(0, heads // 2, two_heads, 0)
    for load in loads[3:]:
        load.wait()
    attended = mixed[...].T
    mid = (rows_ref[...].astype(jnp.float32) + dot32(attended, proj_ref[...])).astype(jnp.bfloat16)
    mid32 = mid.astype(jnp.float32)
    normed = layer_norm(mid32, gain_ref[...], shift_ref[...]).astype(jnp.bfloat16)
    pre = dot32(normed, fc1_ref[...]) + fc1_bias_ref[...]
    hidden = (0.5 * pre * (1.0 + lax.erf(pre * (0.5**0.5)))).astype(jnp.bfloat16)
    rows_ref[...] = (mid32 + dot32(hidden, fc2_ref[...])).astype(jnp.bfloat16)
    save = pltpu.make_async_copy(rows_ref, out_ref, load_sem.at[len(loads)])
    save.start()
    save.wait()


def tail_call(reordered, queries, pairs, ids, proj, gain, shift, fc1, fc1_bias, fc2):
    rows, width = reordered.shape
    count = pairs.shape[0]
    loaded = [
        pairs, queries, ids[None], reordered, proj, gain[None], shift[None], fc1, fc1_bias[None],
        fc2,
    ]
    return pl.pallas_call(
        tail_kernel,
        out_shape=jax.ShapeDtypeStruct((rows, width), jnp.bfloat16),
        in_specs=[pl.BlockSpec(memory_space=pltpu.HBM)] * len(loaded),
        out_specs=pl.BlockSpec(memory_space=pltpu.HBM),
        scratch_shapes=[
            pltpu.VMEM((count, LANES), jnp.int32),
            pltpu.VMEM((count, width), jnp.bfloat16),
            pltpu.VMEM((rows, width), jnp.bfloat16),
            pltpu.VMEM((width, count), jnp.bfloat16),
            pltpu.VMEM((count, rows), jnp.float32),
            pltpu.VMEM((count, rows), jnp.float32),
            pltpu.VMEM((width, rows), jnp.bfloat16),
            pltpu.SemaphoreType.DMA((len(loaded) + 1,)),
        ]
        + [pltpu.VMEM(array.shape, array.dtype) for array in loaded],
        compiler_params=pltpu.CompilerParams(vmem_limit_bytes=VMEM_BYTES),
        name="tail",
    )(*loaded)


def local(
    features,
    neighbours,
    fetch_table,
    hilbert_slot,
    patch_ids,
    conv_weight,
    cpe_weight,
    cpe_bias,
    cpe_gain,
    cpe_shift,
    norm1_gain,
    norm1_shift,
    query_weight,
    pair_weight,
    proj_weight,
    norm2_gain,
    norm2_shift,
    fc1_weight,
    fc1_bias,
    fc2_weight,
):
    rows_dev = features.shape[0]
    reordered, query_rows, all_pairs = front_call(
        fetch_table, hilbert_slot, neighbours, features, conv_weight, cpe_weight,
        cpe_bias, cpe_gain, cpe_shift, norm1_gain, norm1_shift, query_weight, pair_weight,
    )
    return tail_call(
        reordered, query_rows, all_pairs, patch_ids, proj_weight, norm2_gain,
        norm2_shift, fc1_weight, fc1_bias, fc2_weight,
    )


def solution(mesh):
    return jax.shard_map(
        local,
        mesh=mesh,
        in_specs=(
            P(("groups", "region", "slab", "chip"), None),
            P(None, ("groups", "region", "slab", "chip")),
            P("groups", "slab", "chip", None, None),
            P(("groups", "region", "slab", "chip")),
            P(("groups", "region", "slab")),
            P(None, None, "chip"),
            P(),
            P(),
            P(),
            P(),
            P(),
            P(),
            P(),
            P(),
            P(),
            P(),
            P(),
            P(),
            P(),
            P(),
        ),
        out_specs=P(("groups", "region", "slab", "chip"), None),
        check_vma=False,
    )
```

```python
import functools

import jax
import jax.numpy as jnp
from jax import lax
from jax.experimental import pallas as pl
from jax.experimental.pallas import tpu as pltpu
from jax.sharding import PartitionSpec as P

HEAD_DIM = 16
BLOCK = 64
HALO_B = 2
LANES = 128
VMEM_BYTES = 64 * 1024 * 1024


def layer_norm(values, gain, shift):
    mean = jnp.mean(values, axis=-1, keepdims=True)
    centered = values - mean
    var = jnp.mean(centered * centered, axis=-1, keepdims=True)
    return centered * lax.rsqrt(var + 1e-05) * gain + shift


def dot32(a, b):
    return jnp.dot(a, b, preferred_element_type=jnp.float32)


def front_kernel(
    sizes, table_ref, slot_ref, half_ref, *refs,
):
    sources_hbm, results = refs[:10], refs[10:13]
    (
        codes, marks, acc, held, rest, weight, fetch_out, label_out, label_in, moved_out,
        moved_in, pairs_in, fetch_sem, halo_sem, weight_sem, label_sem, moved_sem, pairs_sem,
        local_sem, load_sem, rows_ref, query_ref, pairs_ref, save_sem,
    ) = refs[13:37]
    loads = [
        pltpu.make_async_copy(source, held_here, load_sem.at[i])
        for i, (source, held_here) in enumerate(zip(sources_hbm, refs[37:]))
    ]
    for load in loads:
        load.start()
    (
        feat_ref, nbr_ref, lin_ref, bias_ref, gain_ref, shift_ref, gain1_ref, shift1_ref, wq_ref,
        wp_ref,
    ) = refs[37:]
    regions, slabs, chips, slots, cap = sizes
    offsets = weight.shape[0]
    rows, width = feat_ref.shape
    count = rows // BLOCK
    halo = HALO_B * BLOCK
    own_tiles = rows // LANES
    rest_tiles = rest.shape[0] // LANES
    halo_tiles = halo // LANES
    together = 3 if offsets % 3 == 0 else 1
    here, slab, chip = lax.axis_index("region"), lax.axis_index("slab"), lax.axis_index("chip")
    right, left = lax.rem(slab + 1, slabs), lax.rem(slab + slabs - 1, slabs)
    peers = [{"region": lax.rem(here + d, regions)} for d in range(1, regions)]
    mate = {"chip": 1 - chip}

    barrier = pltpu.get_barrier_semaphore()
    for device in peers + [{"slab": right}, {"slab": left}, mate]:
        pl.semaphore_signal(
            barrier, inc=1, device_id=device, device_id_type=pl.DeviceIdType.MESH
        )
    pl.semaphore_wait(barrier, len(peers) + 3)

    def send(src, dst, sems, at, device):
        copy = pltpu.make_async_remote_copy(
            src_ref=src, dst_ref=dst, send_sem=sems.at[0, at], recv_sem=sems.at[1, at],
            device_id=device, device_id_type=pl.DeviceIdType.MESH,
        )
        copy.start()
        return copy

    mine = weight.at[:, :, pl.ds(pl.multiple_of(chip * half_ref.shape[2], LANES), half_ref.shape[2])]
    weight_copy = send(half_ref, mine, weight_sem, 0, mate)
    weight_own = pltpu.make_async_copy(half_ref, mine, local_sem)
    weight_own.start()

    loads[0].wait()

    def chosen(number, ref):
        label = jnp.full((1, width), number.astype(jnp.float32)).astype(jnp.bfloat16)
        block = jnp.zeros((BLOCK, width), jnp.bfloat16)
        for b in range(count):
            block = jnp.where(
                label == jnp.bfloat16(b), ref[b * BLOCK : (b + 1) * BLOCK, :], block
            )
        return block

    fetches = []
    for d in range(regions):
        to = lax.rem(here + d, regions)
        for k in range(slots):
            block = chosen(table_ref[here, 0, 0, to, k], feat_ref)
            if d == 0:
                at = 2 * halo + (here * slots + k) * BLOCK
                rest[pl.ds(pl.multiple_of(at, BLOCK), BLOCK), :] = block
            else:
                fetch_out[d - 1, k * BLOCK : (k + 1) * BLOCK, :] = block
        if d > 0:
            at = pl.multiple_of(2 * halo + here * slots * BLOCK, slots * BLOCK)
            fetches.append(
                send(
                    fetch_out.at[d - 1], rest.at[pl.ds(at, slots * BLOCK)], fetch_sem, d - 1,
                    peers[d - 1],
                )
            )
    low = send(
        feat_ref.at[pl.ds(rows - halo, halo)], rest.at[pl.ds(0, halo)], halo_sem, 0,
        {"slab": right},
    )
    high = send(
        feat_ref.at[pl.ds(0, halo)], rest.at[pl.ds(halo, halo)], halo_sem, 1, {"slab": left}
    )

    placed = [slot_ref[b] for b in range(count)]
    region_of = [lax.div(p, count) for p in placed]
    rank = [
        sum([jnp.where(region_of[a] == region_of[b], 1, 0) for a in range(b)], jnp.int32(0))
        for b in range(count)
    ]
    sources = []
    line = lax.broadcasted_iota(jnp.int32, (16, LANES), 0)
    labels = []
    for d in range(regions):
        to = lax.rem(here + d, regions)
        text = jnp.full((16, LANES), -1, jnp.int32)
        source = []
        for k in range(cap):
            block, label = jnp.int32(0), jnp.int32(-1)
            for b in range(count):
                hit = jnp.logical_and(region_of[b] == to, rank[b] == k)
                block = jnp.where(hit, b, block)
                label = jnp.where(hit, lax.rem(placed[b], count), label)
            source.append(block)
            text = jnp.where(line == k, label, text)
        sources.append(source)
        text = text.astype(jnp.float32).astype(jnp.bfloat16)
        if d == 0:
            label_in[0] = text
        else:
            label_out[d - 1] = text
            labels.append(send(label_out.at[d - 1], label_in.at[d], label_sem, d - 1, peers[d - 1]))

    loads[1].wait()
    numbers = nbr_ref[...].T
    low_part = jnp.bitwise_and(numbers, LANES - 1) + LANES
    high_part = jnp.right_shift(jnp.maximum(numbers, 0), 7)
    coded = jnp.where(numbers >= 0, jnp.left_shift(low_part, high_part), 0).astype(jnp.float32)
    for o in range(offsets):
        codes[o] = jnp.broadcast_to(coded[:, o : o + 1], (rows, LANES)).astype(jnp.bfloat16)
    lane = lax.broadcasted_iota(jnp.int32, (16, LANES), 1) + LANES
    for t in range(own_tiles + rest_tiles):
        marks[t] = jnp.left_shift(lane, t).astype(jnp.float32).astype(jnp.bfloat16)
    one = jnp.ones((rows, LANES), jnp.bfloat16)
    zero = jnp.zeros((rows, LANES), jnp.bfloat16)

    def picks(i, tiles):
        lines = []
        for j in range(together):
            code = codes[i * together + j]
            lines.append(
                jnp.concatenate(
                    [
                        jnp.where(code == jnp.tile(marks[t], (rows // 16, 1)), one, zero)
                        for t in tiles
                    ],
                    axis=1,
                )
            )
        return jnp.concatenate(lines, axis=0)

    def own_step(i, carry):
        pick = picks(i, range(halo_tiles, halo_tiles + own_tiles))
        held[i] = dot32(pick, feat_ref[...]).astype(jnp.bfloat16)
        return carry

    lax.fori_loop(0, offsets // together, own_step, 0)
    acc[...] = jnp.zeros_like(acc)
    for copy in fetches + [low, high, weight_copy] + loads[2:]:
        copy.wait()
    weight_own.wait()
    first = rest[0:halo, :]
    rest[0:halo, :] = jnp.where(slab > 0, first, jnp.zeros_like(first))
    second = rest[halo : 2 * halo, :]
    rest[halo : 2 * halo, :] = jnp.where(slab < slabs - 1, second, jnp.zeros_like(second))
    others = list(range(halo_tiles)) + list(
        range(halo_tiles + own_tiles, own_tiles + rest_tiles)
    )

    def rest_step(i, carry):
        got = dot32(picks(i, others), rest[...]).astype(jnp.bfloat16) + held[i]
        total = acc[...]
        for j in range(together):
            total += dot32(got[j * rows : (j + 1) * rows], weight[i * together + j])
        acc[...] = total
        return carry

    lax.fori_loop(0, offsets // together, rest_step, 0)
    conv = acc[...].astype(jnp.bfloat16)
    lin = dot32(conv, lin_ref[...]) + bias_ref[...]
    rows_ref[...] = (
        feat_ref[...].astype(jnp.float32) + layer_norm(lin, gain_ref[...], shift_ref[...])
    ).astype(jnp.bfloat16)

    moves = []
    for d in list(range(1, regions)) + [0]:
        for k in range(cap):
            block = chosen(sources[d][k], rows_ref)
            if d == 0:
                moved_in[0, k * BLOCK : (k + 1) * BLOCK, :] = block
            else:
                moved_out[d - 1, k * BLOCK : (k + 1) * BLOCK, :] = block
        if d > 0:
            moves.append(send(moved_out.at[d - 1], moved_in.at[d], moved_sem, d - 1, peers[d - 1]))
    for copy in labels + moves:
        copy.wait()
    for j in range(count):
        block = jnp.zeros((BLOCK, width), jnp.bfloat16)
        for d in range(regions):
            for k in range(cap):
                label = jnp.tile(label_in[d, k : k + 1, :], (1, width // LANES))
                block = jnp.where(
                    label == jnp.bfloat16(j), moved_in[d, k * BLOCK : (k + 1) * BLOCK, :], block
                )
        rows_ref[j * BLOCK : (j + 1) * BLOCK, :] = block

    normed = layer_norm(
        rows_ref[...].astype(jnp.float32), gain1_ref[...], shift1_ref[...]
    ).astype(jnp.bfloat16)
    ours = pl.ds(pl.multiple_of(chip * rows, rows), rows)
    theirs = pl.ds(pl.multiple_of((1 - chip) * rows, rows), rows)
    pairs = dot32(normed, wp_ref[...]).astype(jnp.bfloat16)
    pairs_in[ours, :] = pairs
    pairs_copy = send(pairs_in.at[ours], pairs_in.at[ours], pairs_sem, 0, mate)
    pairs_ref[ours, :] = pairs
    query = dot32(normed, wq_ref[...]).astype(jnp.bfloat16)
    query_ref[...] = query * jnp.bfloat16(HEAD_DIM ** (-0.5))
    saves = [
        pltpu.make_async_copy(rows_ref, results[0], save_sem.at[0]),
        pltpu.make_async_copy(query_ref, results[1], save_sem.at[1]),
        pltpu.make_async_copy(pairs_ref.at[ours], results[2].at[ours], save_sem.at[2]),
    ]
    for save in saves:
        save.start()
    pairs_copy.wait()
    saves.append(
        pltpu.make_async_copy(pairs_in.at[theirs], results[2].at[theirs], save_sem.at[3])
    )
    saves[3].start()
    for save in saves:
        save.wait()


def front_call(
    table, hilbert_slot, neighbours, features, half, lin, bias, gain, shift, gain1, shift1, wq, wp
):
    rows, width = features.shape
    offsets = half.shape[0]
    regions, slabs, chips = (lax.axis_size(axis) for axis in ("region", "slab", "chip"))
    slots = table.shape[4]
    count = rows // BLOCK
    cap = max(1, 2 * count // regions)
    together = 3 if offsets % 3 == 0 else 1
    rest_rows = (2 * HALO_B + regions * slots) * BLOCK
    tiles = (rows + rest_rows) // LANES
    smem = pl.BlockSpec(memory_space=pltpu.SMEM)
    loaded = [
        features, neighbours, lin, bias[None], gain[None], shift[None], gain1[None],
        shift1[None], wq, wp,
    ]
    shape = jax.ShapeDtypeStruct
    return pl.pallas_call(
        functools.partial(front_kernel, (regions, slabs, chips, slots, cap)),
        out_shape=[
            shape((rows, width), jnp.bfloat16),
            shape((rows, width), jnp.bfloat16),
            shape((chips * rows, 2 * width), jnp.bfloat16),
        ],
        in_specs=[smem, smem] + [pl.BlockSpec(memory_space=pltpu.HBM)] * (1 + len(loaded)),
        out_specs=[pl.BlockSpec(memory_space=pltpu.HBM)] * 3,
        scratch_shapes=[
            pltpu.VMEM((offsets, rows, LANES), jnp.bfloat16),
            pltpu.VMEM((tiles, 16, LANES), jnp.bfloat16),
            pltpu.VMEM((rows, width), jnp.float32),
            pltpu.VMEM((offsets // together, together * rows, width), jnp.bfloat16),
            pltpu.VMEM((rest_rows, width), jnp.bfloat16),
            pltpu.VMEM((offsets, width, chips * half.shape[2]), jnp.bfloat16),
            pltpu.VMEM((regions - 1, slots * BLOCK, width), jnp.bfloat16),
            pltpu.VMEM((regions - 1, 16, LANES), jnp.bfloat16),
            pltpu.VMEM((regions, 16, LANES), jnp.bfloat16),
            pltpu.VMEM((regions - 1, cap * BLOCK, width), jnp.bfloat16),
            pltpu.VMEM((regions, cap * BLOCK, width), jnp.bfloat16),
            pltpu.VMEM((chips * rows, 2 * width), jnp.bfloat16),
            pltpu.SemaphoreType.DMA((2, regions - 1)),
            pltpu.SemaphoreType.DMA((2, 2)),
            pltpu.SemaphoreType.DMA((2, 1)),
            pltpu.SemaphoreType.DMA((2, regions - 1)),
            pltpu.SemaphoreType.DMA((2, regions - 1)),
            pltpu.SemaphoreType.DMA((2, 1)),
            pltpu.SemaphoreType.DMA,
            pltpu.SemaphoreType.DMA((len(loaded),)),
            pltpu.VMEM((rows, width), jnp.bfloat16),
            pltpu.VMEM((rows, width), jnp.bfloat16),
            pltpu.VMEM((chips * rows, 2 * width), jnp.bfloat16),
            pltpu.SemaphoreType.DMA((4,)),
        ]
        + [pltpu.VMEM(array.shape, array.dtype) for array in loaded],
        compiler_params=pltpu.CompilerParams(
            vmem_limit_bytes=VMEM_BYTES, collective_id=0, has_side_effects=True
        ),
        name="front",
    )(table, hilbert_slot, half, *loaded)


def tail_kernel(
    *refs,
):
    out_ref, ids, key_marks, own_marks, values, even, odd, mixed, load_sem = refs[10:19]
    loads = [
        pltpu.make_async_copy(source, held, load_sem.at[i])
        for i, (source, held) in enumerate(zip(refs[:10], refs[19:]))
    ]
    for load in loads:
        load.start()
    (
        pairs_ref, query_ref, ids_ref, rows_ref, proj_ref, gain_ref, shift_ref, fc1_ref,
        fc1_bias_ref, fc2_ref,
    ) = refs[19:]
    loads[2].wait()
    rows, width = rows_ref.shape
    count = pairs_ref.shape[0]
    heads = width // HEAD_DIM
    zero = jnp.zeros((), jnp.bfloat16)
    lane = lax.broadcasted_iota(jnp.int32, (1, width), 1)
    scan = jnp.bitwise_and(lane, LANES - 1)
    ids[...] = jnp.broadcast_to(ids_ref[...], (LANES, count)).T
    column = jnp.tile(ids[...], (1, width // LANES))
    key_marks[...] = jnp.where(column == scan, 1.0, 0.0).astype(jnp.bfloat16)
    start = pl.multiple_of(lax.axis_index("chip") * rows, rows)
    own = jnp.tile(ids[pl.ds(start, rows), :], (1, width // LANES))
    own_marks[...] = jnp.where(own == scan, 0.0, -1e30).astype(jnp.bfloat16)
    for load in loads[:2]:
        load.wait()
    values[...] = pairs_ref[:, width:].T

    def score(h, out):
        mine = lane // HEAD_DIM == h
        query = jnp.where(mine, query_ref[...], own_marks[...])
        keys = jnp.where(mine, pairs_ref[:, :width], key_marks[...])
        out[...] = lax.dot_general(
            keys, query, (((1,), (1,)), ((), ())), preferred_element_type=jnp.float32
        )

    def attend(h, scores):
        held = scores[...]
        top = jnp.max(held, axis=0, keepdims=True)
        expo = jnp.exp(held - top)
        total = jnp.sum(expo, axis=0, keepdims=True)
        weights = expo.astype(jnp.bfloat16)
        at = pl.ds(pl.multiple_of(h * HEAD_DIM, HEAD_DIM), HEAD_DIM)
        mixed[at, :] = (dot32(values[at, :], weights) * (1.0 / total)).astype(jnp.bfloat16)

    score(0, even)

    def two_heads(i, carry):
        h = 2 * i
        score(h + 1, odd)
        attend(h, even)
        score(jnp.minimum(h + 2, heads - 1), even)
        attend(h + 1, odd)
        return carry

    lax.fori_loop(0, heads // 2, two_heads, 0)
    for load in loads[3:]:
        load.wait()
    attended = mixed[...].T
    mid = (rows_ref[...].astype(jnp.float32) + dot32(attended, proj_ref[...])).astype(jnp.bfloat16)
    mid32 = mid.astype(jnp.float32)
    normed = layer_norm(mid32, gain_ref[...], shift_ref[...]).astype(jnp.bfloat16)
    pre = dot32(normed, fc1_ref[...]) + fc1_bias_ref[...]
    hidden = (0.5 * pre * (1.0 + lax.erf(pre * (0.5**0.5)))).astype(jnp.bfloat16)
    rows_ref[...] = (mid32 + dot32(hidden, fc2_ref[...])).astype(jnp.bfloat16)
    save = pltpu.make_async_copy(rows_ref, out_ref, load_sem.at[len(loads)])
    save.start()
    save.wait()


def tail_call(reordered, queries, pairs, ids, proj, gain, shift, fc1, fc1_bias, fc2):
    rows, width = reordered.shape
    count = pairs.shape[0]
    loaded = [
        pairs, queries, ids[None], reordered, proj, gain[None], shift[None], fc1, fc1_bias[None],
        fc2,
    ]
    return pl.pallas_call(
        tail_kernel,
        out_shape=jax.ShapeDtypeStruct((rows, width), jnp.bfloat16),
        in_specs=[pl.BlockSpec(memory_space=pltpu.HBM)] * len(loaded),
        out_specs=pl.BlockSpec(memory_space=pltpu.HBM),
        scratch_shapes=[
            pltpu.VMEM((count, LANES), jnp.int32),
            pltpu.VMEM((count, width), jnp.bfloat16),
            pltpu.VMEM((rows, width), jnp.bfloat16),
            pltpu.VMEM((width, count), jnp.bfloat16),
            pltpu.VMEM((count, rows), jnp.float32),
            pltpu.VMEM((count, rows), jnp.float32),
            pltpu.VMEM((width, rows), jnp.bfloat16),
            pltpu.SemaphoreType.DMA((len(loaded) + 1,)),
        ]
        + [pltpu.VMEM(array.shape, array.dtype) for array in loaded],
        compiler_params=pltpu.CompilerParams(vmem_limit_bytes=VMEM_BYTES),
        name="tail",
    )(*loaded)


def local(
    features,
    neighbours,
    fetch_table,
    hilbert_slot,
    patch_ids,
    conv_weight,
    cpe_weight,
    cpe_bias,
    cpe_gain,
    cpe_shift,
    norm1_gain,
    norm1_shift,
    query_weight,
    pair_weight,
    proj_weight,
    norm2_gain,
    norm2_shift,
    fc1_weight,
    fc1_bias,
    fc2_weight,
):
    rows_dev = features.shape[0]
    reordered, query_rows, all_pairs = front_call(
        fetch_table, hilbert_slot, neighbours, features, conv_weight, cpe_weight,
        cpe_bias, cpe_gain, cpe_shift, norm1_gain, norm1_shift, query_weight, pair_weight,
    )
    return tail_call(
        reordered, query_rows, all_pairs, patch_ids, proj_weight, norm2_gain,
        norm2_shift, fc1_weight, fc1_bias, fc2_weight,
    )


def solution(mesh):
    return jax.shard_map(
        local,
        mesh=mesh,
        in_specs=(
            P(("groups", "region", "slab", "chip"), None),
            P(None, ("groups", "region", "slab", "chip")),
            P("groups", "slab", "chip", None, None),
            P(("groups", "region", "slab", "chip")),
            P(("groups", "region", "slab")),
            P(None, None, "chip"),
            P(),
            P(),
            P(),
            P(),
            P(),
            P(),
            P(),
            P(),
            P(),
            P(),
            P(),
            P(),
            P(),
            P(),
        ),
        out_specs=P(("groups", "region", "slab", "chip"), None),
        check_vma=False,
    )
```
